32 devices in a mesh: section: 2 (over x), dp: 16 (over z, y, core).
Axes of the slice: x: 2, y: 2, z: 4, core: 2. Of those that a mesh axis runs over, the one named last changes fastest.
Arguments:
- rows_in: bfloat16 [2, 192, 256, 384], P('section', 'dp'), may hold values from -6 to 6
- rows_cot: bfloat16 [2, 192, 256, 384], P('section', 'dp'), may hold values from -6 to 6
- counts: int32 [192], P('dp'), may hold values from 32 to 128, as said below
- codes: int32 [192, 128], P('dp'), may hold values from 0 to 4095
- codebook: float32 [4096, 12], replicated, may hold values from -6 to 6
- first_gain: float32 [2, 384], P('section'), may hold values from 0.5 to 1.5
- first_bias: float32 [2, 384], P('section'), may hold values from -1.75 to 1.75
- joint_weight: bfloat16 [2, 384, 1152], P('section'), may hold values from -0.3125 to 0.3125
- mixer_weight: bfloat16 [2, 384, 384], P('section'), may hold values from -2.5 to 2.5
- mixer_bias: float32 [2, 384], P('section'), may hold values from -1.75 to 1.75
- second_gain: float32 [2, 384], P('section'), may hold values from 0.5 to 1.5
- second_bias: float32 [2, 384], P('section'), may hold values from -1.75 to 1.75
- expand_weight: bfloat16 [2, 384, 1536], P('section'), may hold values from -0.3125 to 0.3125
- expand_bias: float32 [2, 1536], P('section'), may hold values from -3 to 3
- reduce_weight: bfloat16 [2, 1536, 384], P('section'), may hold values from -0.15625 to 0.15625
- reduce_bias: float32 [2, 384], P('section'), may hold values from -1.75 to 1.75
- latent_rows: float32 [2, 128, 384], P('section'), may hold values from -6 to 6
- latent_map: bfloat16 [2, 384, 12], P('section'), may hold values from -0.625 to 0.625
Outputs:
- rows_out: bfloat16 [2, 192, 256, 384], P('section', 'dp')
- rows_grad: float32 [2, 192, 256, 384], P('section', 'dp')
- first_gain_grad: float32 [2, 384], P('section')
- first_bias_grad: float32 [2, 384], P('section')
- joint_weight_grad: float32 [2, 384, 1152], P('section')
- mixer_weight_grad: float32 [2, 384, 384], P('section')
- mixer_bias_grad: float32 [2, 384], P('section')
- second_gain_grad: float32 [2, 384], P('section')
- second_bias_grad: float32 [2, 384], P('section')
- expand_weight_grad: float32 [2, 384, 1536], P('section')
- expand_bias_grad: float32 [2, 1536], P('section')
- reduce_weight_grad: float32 [2, 1536, 384], P('section')
- reduce_bias_grad: float32 [2, 384], P('section')
- latent_rows_grad: float32 [2, 128, 384], P('section')
- latent_map_grad: float32 [2, 384, 12], P('section')
The draws below stay inside these ranges and needn't reach their ends.
Inputs may be any that keep to these rules, and one draw needn't show every extreme that they name: `counts`: each image's count is one quarter, one half or all of 128; its first count latents are live.
All inputs are finite; a program needn't handle non-finite values.
Results may differ from the reference program's by a relative error of at most 0.0099.
Values may be sent and summed in bfloat16 or wider, within the bound.
A program may use at most 192 MiB of HBM per device.

```python
import jax
import jax.numpy as jnp
from jax import lax

D = 384
HEADS = 6
HEAD_DIM = 64
FF = 1536
PATCH = 256
LAT = 128
CODE = 12
VOCAB = 4096
IMG_DEV = 12
IMAGES = 192


def draw_counts(key, part):
    key = jax.random.fold_in(key, 11)
    levels = jax.random.randint(key, (IMAGES,), 0, 3)
    values = LAT // 4 * jnp.left_shift(jnp.ones((IMAGES,), jnp.int32), levels)
    values = values.at[0].set(LAT).at[1].set(LAT // 4)
    return values.astype(jnp.int32)


def set_ends(result, key, least, top_value):
    spot = [jax.random.randint(jax.random.fold_in(key, axis), (), 0, length) for axis, length in enumerate(result.shape)]
    widest = result.shape.index(max(result.shape))
    next_to = spot[:widest] + [(spot[widest] + 1) % result.shape[widest]] + spot[widest + 1:]
    return result.at[tuple(spot)].set(least).at[tuple(next_to)].set(top_value)


def block_levels(own_key, shape, cuts, least, largest):
    factor_of = 1.0
    for dim, blocks in cuts:
        heights = jax.random.uniform(jax.random.fold_in(jax.random.fold_in(own_key, 6), dim), (blocks,), jnp.float32, least / len(cuts), largest / len(cuts))
        factor_of = factor_of * jnp.repeat(jnp.exp(heights), shape[dim] // blocks).reshape((-1,) + (1,) * (len(shape) - 1 - dim))
    return factor_of


def scatter_about(own_key, shape, scale, limit, cuts=(), held_as=jnp.bfloat16):
    drawn = scale * jax.random.normal(own_key, shape, jnp.float32)
    if cuts:
        drawn = drawn * block_levels(own_key, shape, cuts, -0.22, 0.18)
    return jnp.clip(drawn, -limit, limit).astype(held_as)


def setup_inputs(seed: int = 0) -> dict:
    arg_keys = jax.random.split(jax.random.key(seed), 19)
    return {
        "rows_in": scatter_about(arg_keys[0], (2, IMAGES, PATCH, D), 1.0, 6.0, ((0, 2), (1, 16))),
        "rows_cot": scatter_about(arg_keys[1], (2, IMAGES, PATCH, D), 1.0, 6.0, ((0, 2), (1, 16))),
        "counts": draw_counts(jax.random.fold_in(arg_keys[18], 71), 0),
        "codes": set_ends(jax.random.randint(arg_keys[3], (IMAGES, LAT), 0, VOCAB), jax.random.fold_in(arg_keys[3], 1), 0, VOCAB - 1).astype(jnp.int32),
        "codebook": scatter_about(arg_keys[4], (VOCAB, CODE), 1.0, 6.0, (), jnp.float32),
        "first_gain": jnp.clip(0.5 + 1.0 * jax.random.uniform(arg_keys[5], (2, D), jnp.float32) ** block_levels(arg_keys[5], (2, D), ((0, 2),), -0.2, 0.2), 0.5, 1.5),
        "first_bias": scatter_about(arg_keys[6], (2, D), 0.3, 1.75, ((0, 2),), jnp.float32),
        "joint_weight": scatter_about(arg_keys[7], (2, D, 3 * D), D ** -0.5, 0.3125, ((0, 2),)),
        "mixer_weight": scatter_about(arg_keys[8], (2, D, D), (D // 64) ** -0.5, 2.5, ((0, 2),)),
        "mixer_bias": scatter_about(arg_keys[9], (2, D), 0.3, 1.75, ((0, 2),), jnp.float32),
        "second_gain": jnp.clip(0.5 + 1.0 * jax.random.uniform(arg_keys[10], (2, D), jnp.float32) ** block_levels(arg_keys[10], (2, D), ((0, 2),), -0.2, 0.2), 0.5, 1.5),
        "second_bias": scatter_about(arg_keys[11], (2, D), 0.3, 1.75, ((0, 2),), jnp.float32),
        "expand_weight": scatter_about(arg_keys[12], (2, D, FF), D ** -0.5, 0.3125, ((0, 2),)),
        "expand_bias": scatter_about(arg_keys[13], (2, FF), 0.5, 3.0, ((0, 2),), jnp.float32),
        "reduce_weight": scatter_about(arg_keys[14], (2, FF, D), FF ** -0.5, 0.15625, ((0, 2),)),
        "reduce_bias": scatter_about(arg_keys[15], (2, D), 0.3, 1.75, ((0, 2),), jnp.float32),
        "latent_rows": scatter_about(arg_keys[16], (2, LAT, D), 1.0, 6.0, ((0, 2),), jnp.float32),
        "latent_map": scatter_about(arg_keys[17], (2, D, CODE), 0.1, 0.625, ((0, 2),)),
    }


commit_weight = 0.25
norm_eps = 1e-05
masked_score = -1e+30
highest = lax.Precision.HIGHEST

@jax.custom_vjp
def low(v):
    return lax.optimization_barrier(v.astype(jnp.bfloat16)).astype(jnp.float32)

@jax.custom_vjp
def low_back(v):
    return v

def low_keep(v):
    return (low(v), None)

def low_pass(kept, grad):
    return (grad,)

def back_keep(v):
    return (v, None)

def back_low(kept, grad):
    return (low(grad),)
low.defvjp(low_keep, low_pass)
low_back.defvjp(back_keep, back_low)

def layer_norm(values, gain, offset):
    center = values - lax.optimization_barrier(jnp.mean(values, -1, keepdims=True))
    spread = lax.optimization_barrier(jnp.mean(center * center, -1, keepdims=True))
    return center * lax.rsqrt(spread + norm_eps) * gain + offset

def block(params, stream, live_keys):
    first_gain, first_bias, joint_weight, mixer_weight, mixer_bias, second_gain, second_bias, expand_weight, expand_bias, reduce_weight, reduce_bias = params
    groups, rows = (stream.shape[0], stream.shape[1])
    width = HEADS * HEAD_DIM
    normed = low(layer_norm(stream, first_gain, first_bias))
    joint = low(low_back(jnp.einsum('nrd,de->nre', normed, joint_weight, precision=highest)))
    queries = joint[:, :, :width].reshape(groups, rows, HEADS, HEAD_DIM)
    key_rows = joint[:, :, width:2 * width].reshape(groups, rows, HEADS, HEAD_DIM)
    value_rows = joint[:, :, 2 * width:].reshape(groups, rows, HEADS, HEAD_DIM)
    scores = low_back(jnp.einsum('nrhk,nchk->nhrc', queries, key_rows, precision=highest) * HEAD_DIM ** (-0.5))
    scores = jnp.where(live_keys[:, None, None, :], scores, masked_score)
    probs = low(jax.nn.softmax(scores, axis=-1))
    mixed = jnp.einsum('nhrc,nchk->nrhk', probs, value_rows, precision=highest).reshape(groups, rows, width)
    mixed = low(low_back(mixed))
    middle = stream + low_back(jnp.einsum('nrd,de->nre', mixed, mixer_weight, precision=highest) + mixer_bias)
    second = low(layer_norm(middle, second_gain, second_bias))
    hidden = low_back(jnp.einsum('nrd,df->nrf', second, expand_weight, precision=highest) + expand_bias)
    active = low(jax.nn.gelu(hidden, approximate=False))
    return middle + low_back(jnp.einsum('nrf,fd->nrd', active, reduce_weight, precision=highest) + reduce_bias)

def encoder(params, rows, lat_rows, projection, live_keys):
    latent_part = jnp.broadcast_to(lat_rows[None], (rows.shape[0], LAT, lat_rows.shape[1]))
    output = block(params, jnp.concatenate([rows, latent_part], 1), live_keys)
    latent_codes = low(jnp.einsum('nld,dc->nlc', low(output[:, PATCH:]), projection, precision=highest))
    return (output[:, :PATCH], latent_codes)

def decoder(params, rows, lat_rows, projection, quant, live_keys):
    embedded = low_back(jnp.einsum('nlc,dc->nld', low(quant), projection, precision=highest))
    output = block(params, jnp.concatenate([rows, lat_rows[None] + embedded], 1), live_keys)
    return output[:, :PATCH]

def reference(rows_in, rows_cot, counts, codes, codebook, first_gain, first_bias, joint_weight, mixer_weight, mixer_bias, second_gain, second_bias, expand_weight, expand_bias, reduce_weight, reduce_bias, latent_rows, latent_map):
    stacked = [weight.astype(jnp.float32) for weight in (first_gain, first_bias, joint_weight, mixer_weight, mixer_bias, second_gain, second_bias, expand_weight, expand_bias, reduce_weight, reduce_bias)]
    enc_params = tuple((weight[0] for weight in stacked))
    dec_params = tuple((weight[1] for weight in stacked))
    lat_float = latent_rows.astype(jnp.float32)
    map_float = latent_map.astype(jnp.float32)
    book = codebook.astype(jnp.float32)
    group = IMG_DEV
    blocks = IMAGES // group

    def split(values):
        return values.reshape((blocks, group) + values.shape[1:])
    inputs = (split(rows_in[0]), split(rows_in[1]), split(rows_cot[0]), split(rows_cot[1]), split(counts), split(codes))

    def step(carry, pieces):
        enc_rows, dec_rows, enc_cot, dec_cot, count_part, code_part = pieces
        quant = jnp.take(book, code_part, axis=0)
        live_lat = lax.broadcasted_iota(jnp.int32, (group, LAT), 1) < count_part[:, None]
        live_keys = jnp.concatenate([jnp.ones((group, PATCH), dtype=bool), live_lat], 1)

        def first(params, rows, lat_rows, projection):
            return encoder(params, rows, lat_rows, projection, live_keys)
        (enc_out, latent_codes), back_first = jax.vjp(first, enc_params, enc_rows.astype(jnp.float32), lat_float[0], map_float[0])

        def second(params, rows, lat_rows, projection, quant_in, codes_in):
            out = decoder(params, rows, lat_rows, projection, quant_in, live_keys)
            diff = codes_in - quant
            return (out, commit_weight * jnp.sum(jnp.where(live_lat[:, :, None], diff * diff, 0.0)))
        (dec_out, commit), back_second = jax.vjp(second, dec_params, dec_rows.astype(jnp.float32), lat_float[1], map_float[1], quant, latent_codes)
        grad_dec, rows_dec, lat_dec, map_dec, grad_quant, grad_direct = back_second((dec_cot.astype(jnp.float32), jnp.ones_like(commit)))
        code_grad = low(grad_quant + grad_direct)
        grad_enc, rows_enc, lat_enc, map_enc = back_first((enc_cot.astype(jnp.float32), code_grad))
        enc_sum, dec_sum, lat_sum, map_sum = carry
        enc_sum = jax.tree.map(jnp.add, enc_sum, grad_enc)
        dec_sum = jax.tree.map(jnp.add, dec_sum, grad_dec)
        lat_sum = lat_sum + jnp.stack([lat_enc, lat_dec])
        map_sum = map_sum + jnp.stack([map_enc, map_dec])
        return ((enc_sum, dec_sum, lat_sum, map_sum), (enc_out, dec_out, rows_enc, rows_dec))
    zero_params = tuple((jnp.zeros_like(weight) for weight in enc_params))
    init = (zero_params, zero_params, jnp.zeros_like(lat_float), jnp.zeros_like(map_float))
    (enc_sum, dec_sum, lat_sum, map_sum), (enc_out, dec_out, rows_enc, rows_dec) = lax.scan(step, init, inputs)
    shape = (IMAGES, PATCH, enc_out.shape[-1])
    rows_out = jnp.stack([enc_out.reshape(shape), dec_out.reshape(shape)]).astype(jnp.bfloat16)
    rows_grad = jnp.stack([rows_enc.reshape(shape), rows_dec.reshape(shape)])
    grads = [jnp.stack([enc_part, dec_part]) for enc_part, dec_part in zip(enc_sum, dec_sum)]
    return (rows_out, rows_grad, grads[0], grads[1], grads[2], grads[3], grads[4], grads[5], grads[6], grads[7], grads[8], grads[9], grads[10], lat_sum, map_sum)
```

```python
import functools

import jax
import jax.numpy as jnp
from jax import lax
from jax.experimental import pallas as pl
from jax.experimental.pallas import tpu as pltpu
from jax.sharding import PartitionSpec as P

HEADS = 6
PAIRS = 3
LANES = 128
CODE_ROWS = 16
GROUP = 256
commit_weight = 0.25
norm_eps = 1e-05
masked_score = -1e30
LOG2E = 1.4426950408889634
MESH = pl.DeviceIdType.MESH
f32 = jnp.float32
bf16 = jnp.bfloat16
VMEM_BYTES = 63 * 1024 * 1024


def dot_nn(a, b):
    return lax.dot_general(a, b, (((1,), (0,)), ((), ())), preferred_element_type=f32)


def dot_nt(a, b):
    return lax.dot_general(a, b, (((1,), (1,)), ((), ())), preferred_element_type=f32)


def dot_tn(a, b):
    return lax.dot_general(a, b, (((0,), (0,)), ((), ())), preferred_element_type=f32)


def stacked_halves(values):
    lane = lax.broadcasted_iota(jnp.int32, (1, LANES), 1)
    low = (lane < LANES // 2).astype(f32)
    return jnp.concatenate([values * low.astype(bf16), values * (1.0 - low).astype(bf16)], 0)


def normalised(values):
    center = values - jnp.mean(values, -1, keepdims=True)
    spread = jnp.mean(center * center, -1, keepdims=True)
    factor = lax.rsqrt(spread + norm_eps)
    return center * factor, factor


def low(value):
    return jnp.asarray(value, bf16)


def gelu_pair(hidden):
    hidden = hidden.astype(bf16)
    square = hidden * hidden
    poly = low(3.63928092e-02) + square * (low(-8.82193757e-05) + square * (low(-3.66000625e-05) + square * low(1.41853336e-06)))
    phi = low(0.5) + low(0.5) * jnp.tanh(hidden * (low(7.97869556e-01) + square * poly))
    bell = jnp.exp2(square * low(-0.5 * LOG2E))
    return hidden * phi, phi + (hidden * low(0.3989422804014327)) * bell


def forward_body(
    is_encoder, image, counts_ref, rows_ref, codes_ref, base_ref, map_ref, book_ref,
    gain1_ref, bias1_ref, wj_ref, wm_ref, biasm_ref, gain2_ref, bias2_ref, we_ref, biase_ref, wr_ref, biasr_ref,
    out_ref, joint_ref, e_ref, rl_ref, mixed_ref, x1_ref, rs_ref, x2_ref, act_ref, dg_ref, latlow_ref, small_ref,
    map_rows, book_parts, quants,
):
    patch, width = rows_ref.shape[2], rows_ref.shape[3]
    rows = joint_ref.shape[1]
    latents = rows - patch
    ff = act_ref.shape[2]
    used = rows if is_encoder else patch
    if is_encoder:
        lat = base_ref[...]
    else:
        @pl.when(lax.rem(image, 2) == 0)
        def _():
            code = jnp.concatenate([codes_ref[pl.ds(image, 1), :], codes_ref[pl.ds(image + 1, 1), :]], 1)
            entry = lax.broadcasted_iota(jnp.int32, (GROUP, 2 * latents), 0)
            within = jnp.where(entry == lax.rem(code, GROUP), 1.0, 0.0).astype(bf16)
            found = dot_nn(book_parts[...], within)
            tall = 3 * CODE_ROWS
            total = jnp.zeros((tall, 2 * latents), f32)
            for group in range(found.shape[0] // tall):
                here = jnp.where(lax.div(code, GROUP) == group, 1.0, 0.0)
                total = total + found[group * tall : (group + 1) * tall] * here
            quants[...] = total[:CODE_ROWS] + total[CODE_ROWS : 2 * CODE_ROWS] + total[2 * CODE_ROWS :]

        quant = jnp.where(lax.rem(image, 2) == 0, quants[:, :latents], quants[:, latents:])
        small_ref[0] = quant
        lat = base_ref[...] + dot_tn(quant.astype(bf16), map_rows[...])
    stream = jnp.concatenate([rows_ref[0, 0].astype(f32), lat], 0)
    xhat, factor1 = normalised(stream)
    x1_ref[0] = xhat.astype(bf16)
    normed = (xhat * gain1_ref[...] + bias1_ref[...]).astype(bf16)
    joint_ref[0] = dot_nn(normed, wj_ref[0]).astype(bf16)
    scale = (width // HEADS) ** -0.5 * LOG2E
    live = lax.broadcasted_iota(jnp.int32, (1, latents), 1) < counts_ref[image]
    mask = jnp.where(live, 0.0, masked_score)
    sums = stacked_halves(jnp.ones((rows, LANES), bf16))
    for pair in range(PAIRS):
        at = pair * LANES
        q = joint_ref[0, :used, at : at + LANES]
        k = joint_ref[0, :, width + at : width + at + LANES]
        v = joint_ref[0, :, 2 * width + at : 2 * width + at + LANES]
        scores = dot_nt(q, stacked_halves(k))
        shares = []
        for half in range(2):
            start = half * rows
            head = scores[:, start : start + patch]
            tail = scores[:, start + patch : start + rows] + mask
            top = jnp.maximum(jnp.max(head, -1, keepdims=True), jnp.max(tail, -1, keepdims=True))
            share = jnp.exp2((jnp.concatenate([head, tail], 1) - top) * scale).astype(bf16)
            e_ref[0, 2 * pair + half, :used] = share
            shares.append(share)
        gathered = dot_nn(jnp.concatenate(shares, 1), jnp.concatenate([stacked_halves(v), sums], 1))
        norm = 1.0 / gathered[:, LANES:]
        rl_ref[0, :used, at : at + LANES] = norm.astype(bf16)
        mixed_ref[0, :used, at : at + LANES] = (gathered[:, :LANES] * norm).astype(bf16)
    middle = stream[:used] + dot_nn(mixed_ref[0, :used], wm_ref[0]) + biasm_ref[...]
    xhat2, factor2 = normalised(middle)
    x2_ref[0, :used] = xhat2.astype(bf16)
    lane = lax.broadcasted_iota(jnp.int32, (used, LANES), 1)
    rs_ref[0, :used] = jnp.where(lane < LANES // 2, factor1[:used], factor2)
    second = (xhat2 * gain2_ref[...] + bias2_ref[...]).astype(bf16)
    cut = 256
    for at in range(0, ff, cut):
        hidden = dot_nn(second, we_ref[0, :, at : at + cut]) + biase_ref[:, at : at + cut]
        active, slope = gelu_pair(hidden)
        act_ref[0, :used, at : at + cut] = active.astype(bf16)
        dg_ref[0, :used, at : at + cut] = slope.astype(bf16)
    output = middle + dot_nn(act_ref[0, :used], wr_ref[0]) + biasr_ref[...]
    out_ref[0, 0] = output[:patch].astype(bf16)
    if is_encoder:
        low = output[patch:].astype(bf16)
        latlow_ref[0] = low
        small_ref[0] = dot_nt(map_rows[...], low)
    else:
        rs_ref[0, used:] = jnp.broadcast_to(factor1[used:], (latents, LANES))


def put_map_rows(map_ref, map_rows):
    map_rows[...] = jnp.zeros_like(map_rows)
    map_rows[: map_ref.shape[0]] = map_ref[...].astype(f32).astype(bf16)


def forward_kernel(*refs):
    image = pl.program_id(0)
    section = lax.axis_index("section")
    map_ref, book_ref, map_rows, book_parts = refs[4], refs[5], refs[-3], refs[-2]

    @pl.when(image == 0)
    def _():
        put_map_rows(map_ref, map_rows)

    @pl.when((image == 0) & (section == 1))
    def _():
        book_parts[...] = jnp.zeros_like(book_parts)
        left = book_ref[...]
        for index in range(3):
            low = left.astype(bf16)
            for group in range(book_ref.shape[1] // GROUP):
                start = (3 * group + index) * CODE_ROWS
                book_parts[start : start + book_ref.shape[0]] = low[:, group * GROUP : (group + 1) * GROUP]
            left = left - low.astype(f32)

    @pl.when(section == 0)
    def _():
        forward_body(True, image, *refs)

    @pl.when(section == 1)
    def _():
        forward_body(False, image, *refs)


def column_sum(values):
    return jnp.sum(values, 0, keepdims=True)


def norm_back(grad, xhat, factor, gain):
    scaled = grad * gain
    along = jnp.mean(scaled * xhat, -1, keepdims=True)
    return factor * (scaled - jnp.mean(scaled, -1, keepdims=True) - xhat * along)


def reach(devices):
    pair = 2 if devices % 2 == 0 else 1
    side = 2 if devices % (2 * pair) == 0 else 1
    line = 4 if devices % (4 * pair * side) == 0 else 1
    return pair, side, line, devices // (pair * side * line)


class Place:
    def __init__(self, sizes):
        self.pair, self.side, self.line, self.blocks = sizes
        me = lax.axis_index("dp")
        self.core = lax.rem(me, self.pair)
        self.flank = lax.rem(me // self.pair, self.side)
        self.spot = lax.rem(me // (self.pair * self.side), self.line)
        self.block = me // (self.pair * self.side * self.line)

    def at(self, core=None, flank=None, spot=None, block=None):
        core = self.core if core is None else core
        flank = self.flank if flank is None else flank
        spot = self.spot if spot is None else spot
        block = self.block if block is None else block
        return {"dp": ((block * self.line + spot) * self.side + flank) * self.pair + core}

    def other_core(self):
        return self.at(core=1 - self.core)

    def other_flank(self):
        return self.at(flank=1 - self.flank)

    def next_spot(self, step):
        return self.at(spot=lax.rem(self.spot + step, self.line))

    def next_block(self, step):
        return self.at(block=lax.rem(self.block + step, self.blocks))

    def others(self):
        found = [self.other_core()] if self.pair > 1 else []
        found += [self.other_flank()] if self.side > 1 else []
        found += [self.next_spot(step) for step in range(1, self.line)]
        return found + [self.next_block(step) for step in range(1, self.blocks)]


class Flow:
    def __init__(self, place, order, own, recv1, recv2, recv3, far3, final, result, send_sem, recv_sem):
        self.result = result
        self.place, self.order, self.own, self.final = place, order, own, final
        self.recv1, self.recv2, self.recv3, self.far3 = recv1, recv2, recv3, far3
        self.send_sem, self.recv_sem = send_sem, recv_sem
        self.dtype = own.dtype
        self.span = own.shape[1] // place.pair
        self.sides = own.shape[0] // place.side
        self.lines = self.sides // place.line
        self.stages = [0, 1, 2, 3, 5, 6, 7] if place.blocks == 1 else [0, 1, 2, 3, 4, 5, 6, 7]

    def copy(self, number, source, target, device):
        return pltpu.make_async_remote_copy(
            src_ref=source, dst_ref=target, send_sem=self.send_sem.at[self.order, number],
            recv_sem=self.recv_sem.at[self.order, number], device_id=device, device_id_type=MESH,
        )

    def cols(self, which):
        return pl.ds(pl.multiple_of(which * self.span, LANES), self.span)

    def side_rows(self, which):
        return pl.ds(pl.multiple_of(which * self.sides, 16), self.sides)

    def line_rows(self, which):
        return pl.ds(pl.multiple_of(which * self.lines, 16), self.lines)

    def final_rows(self):
        return pl.ds(pl.multiple_of(self.place.flank * self.sides + self.place.spot * self.lines, 16), self.lines)

    def deliver(self):
        return pltpu.make_async_copy(self.final, self.result, self.send_sem.at[self.order, 0])

    def sends(self, stage):
        place = self.place
        mine = self.cols(place.core)
        if stage == 0 and place.pair > 1:
            return [self.copy(0, self.own.at[:, self.cols(1 - place.core)], self.recv1, place.other_core())]
        if stage == 1 and place.side > 1:
            return [self.copy(1, self.recv1.at[self.side_rows(1 - place.flank)], self.recv2, place.other_flank())]
        if stage == 2:
            return [
                self.copy(
                    1 + step, self.recv2.at[self.line_rows(lax.rem(place.spot + step, place.line))], self.recv3.at[step - 1],
                    place.next_spot(step),
                )
                for step in range(1, place.line)
            ]
        if stage == 3:
            spot = self.far3.at[place.block]
            return [self.copy(4 + step, spot, spot, place.next_block(step)) for step in range(1, place.blocks)]
        if stage == 4:
            region = self.final.at[self.final_rows(), mine]
            return [self.copy(10 + step, region, region, place.next_spot(step)) for step in range(1, place.line)]
        if stage == 5 and place.side > 1:
            region = self.final.at[self.side_rows(place.flank), mine]
            return [self.copy(8, region, region, place.other_flank())]
        if stage == 6 and place.pair > 1:
            region = self.final.at[:, mine]
            return [self.copy(9, region, region, place.other_core())]
        return []

    def settle(self, stage):
        place = self.place
        mine = self.cols(place.core)
        for copy in self.sends(stage):
            copy.wait_recv()
        if stage == 0:
            total = self.own[:, mine].astype(f32)
            if place.pair > 1:
                total = total + self.recv1[...].astype(f32)
            self.recv1[...] = total.astype(self.dtype)
        elif stage == 1:
            total = self.recv1[self.side_rows(place.flank)].astype(f32)
            if place.side > 1:
                total = total + self.recv2[...].astype(f32)
            self.recv2[...] = total.astype(self.dtype)
        elif stage == 2:
            total = self.recv2[self.line_rows(place.spot)].astype(f32)
            for step in range(1, place.line):
                total = total + self.recv3[step - 1].astype(f32)
            if place.blocks > 1:
                self.far3[place.block] = total.astype(self.dtype)
            else:
                self.final[self.final_rows(), mine] = total.astype(self.dtype)
        elif stage == 3 and place.blocks > 1:
            total = self.far3[0].astype(f32)
            for index in range(1, place.blocks):
                total = total + self.far3[index].astype(f32)
            self.final[self.final_rows(), mine] = total.astype(self.dtype)

    def advance(self, turn):
        stage = self.stages[turn]
        if stage > 0:
            self.settle(stage - 1)
        if stage == 3 and self.place.blocks == 1:
            stage = 4
        for copy in self.sends(stage):
            copy.start()
        if stage == 7:
            for copy in self.sends(0):
                copy.wait_send()
            self.deliver().start()

    def drain(self):
        for stage in range(1, 7):
            if stage != 3 or self.place.blocks > 1:
                for copy in self.sends(stage):
                    copy.wait_send()
        self.deliver().wait()


LINK, CORE_LINK, LATENCY, POINT, TURN = 100e3, 300e3, 0.8, 0.95, 0.7


def planned(early, late, points, blocks):
    busy, state = {}, {}

    def enter(names, time):
        for name, size in names:
            uses = [("core", size / 2 / CORE_LINK), ("side", size / 2 / LINK), ("line", size / 2 / LINK)]
            if blocks > 1:
                uses.append(("far", size / 4 / LINK))
            state[name] = [0, time, uses + uses[2::-1]]

    def left(name):
        return state[name][0] <= len(state[name][2])

    def turn(name, time):
        entry = state[name]
        if entry[0] < len(entry[2]):
            link, span = entry[2][entry[0]]
            busy[link] = max(busy.get(link, 0.0), time) + span
            entry[1] = busy[link] + LATENCY
        entry[0] += 1
        return entry[0] - 1, time + TURN

    table, rest, time = [], [], 0.0
    enter(early, time)
    for _ in range(points):
        row = []
        for name in state:
            if left(name) and state[name][1] <= time:
                number, time = turn(name, time)
                row.append((name, number))
        table.append(row)
        time += POINT
    enter(late, time)
    while any(left(name) for name in state):
        name = min((state[name][1], name) for name in state if left(name))[1]
        number, time = turn(name, max(time, state[name][1]))
        rest.append((name, number))
    return table, rest


FIRST_GAIN, FIRST_BIAS, MIXER_BIAS, SECOND_GAIN, SECOND_BIAS, REDUCE_BIAS, EXPAND_BIAS, LATENT_MAP = 0, 1, 2, 3, 4, 5, 6, 16


def add_row(vectors, row, values):
    vectors[row : row + 1] += column_sum(values)


def branch_back(
    is_encoder, first, counts_ref, cot_ref, act_ref, latlow_ref, small_ref,
    acc_r, vectors, branch_keep, left_t, map_rows, code_in, code_copy,
):
    count, patch, width = cot_ref.shape[1:]
    rows = act_ref.shape[1]
    latents = rows - patch
    ff = act_ref.shape[2]
    used = rows if is_encoder else patch
    tall = count * used
    cot = cot_ref[0]
    if is_encoder:
        branches = []
        for index in range(count):
            image = first + index
            code_copy(image).wait_recv()
            live = lax.broadcasted_iota(jnp.int32, (1, latents), 1) < counts_ref[image]
            weight = jnp.where(live, 2.0 * commit_weight, 0.0)
            codes = (code_in[image] + weight * small_ref[index].astype(bf16).astype(f32)).astype(bf16)
            vectors[LATENT_MAP : LATENT_MAP + CODE_ROWS] += dot_nn(codes, latlow_ref[index])
            lat_cot = dot_tn(codes, map_rows[...])
            branches += [cot[index], lat_cot.astype(bf16)]
        branch = jnp.concatenate(branches, 0)
    else:
        branch = cot.reshape(tall, width)
    add_row(vectors, REDUCE_BIAS, branch.astype(f32))
    branch_keep[:tall] = branch
    left_t[0, :, :tall] = branch.T
    cut = 512
    for at in range(0, ff, cut):
        span = slice(at, at + cut)
        acc_r[:, span] += dot_nn(left_t[0, :, :tall], act_ref[:, :used, span].reshape(tall, cut))


def feed_forward_back(
    is_encoder, first, dg_ref, x2_ref, rs_ref, gain2_ref, bias2_ref, wm_ref, we_ref, wr_ref,
    vectors, hidden_sums, gmid_keep, pull_keep, ghid, branch_keep, left_t,
):
    count, rows, width = x2_ref.shape
    ff = dg_ref.shape[2]
    used = rows if is_encoder else rows * 2 // 3
    tall = count * used
    branch = branch_keep[:tall]
    grad_out = branch.astype(f32)
    xhat2 = x2_ref[:, :used].reshape(tall, width).astype(f32)
    second = (xhat2 * gain2_ref[...] + bias2_ref[...]).astype(bf16)
    left_t[1, :, :tall] = second.T
    cut = 512
    for at in range(0, ff, cut):
        span = slice(at, at + cut)
        grad_active = dot_nt(branch, wr_ref[0, span, :])
        grad_hidden = grad_active * dg_ref[:, :used, span].reshape(tall, cut).astype(f32)
        hidden_sums[:, span] += column_sum(grad_hidden)
        ghid[:tall, span] = grad_hidden.astype(bf16)
    grad_second = dot_nt(ghid[:tall], we_ref[0])
    add_row(vectors, SECOND_BIAS, grad_second)
    add_row(vectors, SECOND_GAIN, grad_second * xhat2)
    factor2 = rs_ref[:, :used, LANES // 2 : LANES // 2 + 1].reshape(tall, 1)
    grad_middle = norm_back(grad_second, xhat2, factor2, gain2_ref[...]) + grad_out
    grad_mixer = grad_middle.astype(bf16)
    add_row(vectors, MIXER_BIAS, grad_mixer.astype(f32))
    pulled = dot_nt(grad_mixer, wm_ref[0]).astype(bf16)
    ring = gmid_keep.shape[0]
    for index in range(count):
        spot = lax.rem(first + index, ring)
        span = slice(index * used, (index + 1) * used)
        gmid_keep[spot, :used] = grad_mixer[span]
        pull_keep[spot, :used] = pulled[span]


def feed_forward_gradients(is_encoder, first, mixed_ref, acc_e, acc_m, gmid_keep, ghid, left_t):
    count, rows = mixed_ref.shape[:2]
    ff = acc_e.shape[1]
    used = rows if is_encoder else rows * 2 // 3
    tall = count * used
    width = acc_m.shape[0]
    cut = 512
    for at in range(0, ff, cut):
        span = slice(at, at + cut)
        acc_e[:, span] += dot_nn(left_t[1, :, :tall], ghid[:tall, span])
    ring = gmid_keep.shape[0]
    grad_mixer = jnp.concatenate([gmid_keep[lax.rem(first + index, ring), :used] for index in range(count)], 0)
    acc_m[...] += dot_tn(mixed_ref[:, :used].reshape(tall, width), grad_mixer)


def attention_back(is_encoder, image, pairs, joint_ref, e_ref, rl_ref, mixed_ref, pull_keep, gjoints):
    rows, width = mixed_ref.shape[1:]
    gjoint = gjoints.at[lax.rem(image, 2)]
    used = rows if is_encoder else joint_patch(gjoint)
    spot = lax.rem(image, pull_keep.shape[0])
    scale = (width // HEADS) ** -0.5
    half = LANES // 2
    lane = lax.broadcasted_iota(jnp.int32, (used, LANES), 1)

    def own_parts(left, rights):
        made = dot_nn(left.T, jnp.concatenate(rights, 1))
        return jnp.concatenate([made[:half, :rows], made[half:, rows:]], 0)

    for pair in pairs:
        at = pair * LANES
        q = joint_ref[0, :used, at : at + LANES]
        k = joint_ref[0, :, width + at : width + at + LANES]
        v = joint_ref[0, :, 2 * width + at : 2 * width + at + LANES]
        pulled = pull_keep[spot, :used, at : at + LANES].astype(f32)
        pulled = pulled * (rl_ref[0, :used, at : at + LANES].astype(f32) * scale)
        pulled_low = pulled.astype(bf16)
        matched = pulled * mixed_ref[0, :used, at : at + LANES].astype(f32)
        matched_first = jnp.where(lane < half, matched, 0.0)
        shifts = (jnp.sum(matched_first, -1, keepdims=True), jnp.sum(matched - matched_first, -1, keepdims=True))
        grad_probs = dot_nt(pulled_low, stacked_halves(v))
        shares, grads = [], []
        for index in range(2):
            share = e_ref[0, 2 * pair + index, :used]
            shares.append(share)
            grads.append(share * (grad_probs[:, index * rows : (index + 1) * rows] - shifts[index]).astype(bf16))
        gjoint[:used, at : at + LANES] = dot_nn(jnp.concatenate(grads, 1), stacked_halves(k)).astype(bf16)
        gjoint[:, width + at : width + at + LANES] = own_parts(q, grads).astype(bf16).T
        gjoint[:, 2 * width + at : 2 * width + at + LANES] = (own_parts(pulled_low, shares) * (1.0 / scale)).astype(bf16).T
    if not is_encoder:
        gjoint[used:, :width] = jnp.zeros((rows - used, width), bf16)


def joint_patch(gjoint):
    return gjoint.shape[0] * 2 // 3


def first_norm_back(
    is_encoder, image, counts_ref, x1_ref, rs_ref, small_ref, gain1_ref, bias1_ref, wj_ref,
    acc_j, vectors, latent_sums, gmid_keep, gjoints, normed_t, rows_buf, map_rows, code_out, rows_wait,
):
    gjoint = gjoints.at[lax.rem(image, 2)]
    rows, width = x1_ref.shape[1:]
    patch = rows_buf.shape[1]
    latents = rows - patch
    used = rows if is_encoder else patch
    spot = lax.rem(image, gmid_keep.shape[0])
    xhat1 = x1_ref[0].astype(f32)
    normed = (xhat1 * gain1_ref[...] + bias1_ref[...]).astype(bf16)
    grad_normed = dot_nt(gjoint[...], wj_ref[0])
    if is_encoder:
        acc_j[...] += dot_nn(normed.T, gjoint[...])
    else:
        normed_t[lax.rem(image, 2)] = normed.T
    add_row(vectors, FIRST_BIAS, grad_normed)
    add_row(vectors, FIRST_GAIN, grad_normed * xhat1)
    grad_stream = norm_back(grad_normed, xhat1, rs_ref[0, :, 0:1], gain1_ref[...])
    grad_middle = gmid_keep[spot, :used].astype(f32)
    rows_wait(image)
    rows_buf[lax.rem(image, rows_buf.shape[0])] = (grad_stream[:patch] + grad_middle[:patch]).astype(bf16)
    grad_lat = grad_stream[patch:]
    if is_encoder:
        grad_lat = grad_lat + grad_middle[patch:]
    else:
        embed = grad_lat.astype(bf16)
        quant = small_ref[0]
        vectors[LATENT_MAP : LATENT_MAP + CODE_ROWS] += dot_nn(quant.astype(bf16), embed)
        live = lax.broadcasted_iota(jnp.int32, (1, latents), 1) < counts_ref[image]
        weight = jnp.where(live, 2.0 * commit_weight, 0.0)
        code_out[image] = dot_nt(map_rows[...], embed) - weight * quant
    latent_sums[...] += grad_lat


def ahead(images):
    return images // 2 - 1


def put_columns(targets, start, blocks):
    edges = [0]
    for target in targets:
        edges.append(edges[-1] + target.shape[1])
    for block in blocks:
        stop = start + block.shape[1]
        for target, low, high in zip(targets, edges[:-1], edges[1:]):
            left, right = max(low, start), min(high, stop)
            if left < right:
                target[:, left - low : right - low] = block[:, left - start : right - start]
        start = stop


def columns(sources, start, stop):
    found, low = [], 0
    for source in sources:
        high = low + source.shape[1]
        left, right = max(low, start), min(high, stop)
        if left < right:
            found.append(source[:, left - low : right - low])
        low = high
    return found[0] if len(found) == 1 else jnp.concatenate(found, 1)


def backward_kernel(
    sizes, counts_ref,
    cot_ref, act_ref, dg_ref, x2_ref, rs2_ref, mixed2_ref, latlow_ref, small2_ref,
    joint_a, e_a, rl_a, x1_a, mixed_a, rs_a, small_a, joint_b, e_b, rl_b, x1_b,
    map_ref, gain1_ref, bias1_ref, wj_ref, wm_ref, gain2_ref, bias2_ref, we_ref, wr_ref,
    rows_out, out_0, out_1, out_2, out_3,
    acc_r, acc_e, acc_j, acc_m, vectors, hidden_sums, latent_sums, gmid_keep, pull_keep, ghid, branch_keep, left_t, gjoints, normed_t, rows_buf, map_rows,
    code_in, code_out, code_send, code_recv, rows_sem, send_sem, recv_sem, *buffers,
):
    step = pl.program_id(0)
    steps = pl.num_programs(0)
    images = code_in.shape[0]
    half, early_images = images // 2, ahead(images)
    slots = rows_buf.shape[0]
    width = acc_m.shape[0]
    outs = (out_0, out_1, out_2, out_3)
    section = lax.axis_index("section")
    encoder, decoder = section == 0, section == 1
    partner = {"section": 1 - section}
    place = Place(sizes)
    others = place.others()
    barrier = pltpu.get_barrier_semaphore()

    def code_copy(index):
        return pltpu.make_async_remote_copy(
            src_ref=code_out.at[index], dst_ref=code_in.at[index], send_sem=code_send.at[index],
            recv_sem=code_recv.at[index], device_id=partner, device_id_type=MESH,
        )

    def rows_copy(index):
        return pltpu.make_async_copy(rows_buf.at[lax.rem(index, slots)], rows_out.at[0, index], rows_sem.at[index])

    def rows_wait(image):
        @pl.when(image >= slots)
        def _():
            rows_copy(image - slots).wait()

    @pl.when(step == 0)
    def _():
        for device in [partner] + others:
            pl.semaphore_signal(barrier, inc=1, device_id=device, device_id_type=MESH)
        put_map_rows(map_ref, map_rows)
        for ref in (acc_r, acc_e, acc_j, acc_m, vectors, hidden_sums, latent_sums):
            ref[...] = jnp.zeros_like(ref)

    branch_args = (counts_ref, cot_ref, act_ref, latlow_ref, small2_ref)
    branch_args += (acc_r, vectors, branch_keep, left_t, map_rows, code_in, code_copy)
    first_args = (dg_ref, x2_ref, rs2_ref, gain2_ref, bias2_ref, wm_ref, we_ref, wr_ref)
    first_args += (vectors, hidden_sums, gmid_keep, pull_keep, ghid, branch_keep, left_t)
    weight_args = (mixed2_ref, acc_e, acc_m, gmid_keep, ghid, left_t)
    norm_args = (gain1_ref, bias1_ref, wj_ref)
    norm_args += (acc_j, vectors, latent_sums, gmid_keep, gjoints, normed_t, rows_buf, map_rows, code_out, rows_wait)
    set_a = (joint_a, e_a, rl_a, mixed_a), (x1_a, rs_a, small_a)
    pair = [[ref.at[pl.ds(index, 1)] for ref in (mixed2_ref, rs2_ref, small2_ref)] for index in range(2)]
    pair_a = (joint_a, e_a, rl_a, pair[0][0]), (x1_a, pair[0][1], pair[0][2])
    pair_b = (joint_b, e_b, rl_b, pair[1][0]), (x1_b, pair[1][1], pair[1][2])

    def attention(is_encoder, image, refs, pairs=range(PAIRS)):
        attention_back(is_encoder, image, pairs, *refs[0], pull_keep, gjoints)

    def norm(is_encoder, image, refs):
        first_norm_back(is_encoder, image, counts_ref, *refs[1], *norm_args)
        rows_copy(image).start()

    def joint_gradient():
        left = jnp.concatenate([normed_t[0], normed_t[1]], 1)
        acc_j[...] += dot_nn(left, gjoints[...].reshape(2 * gjoints.shape[1], gjoints.shape[2]))

    image = early_images + step - half

    @pl.when(encoder & (step < half) & (image >= 0))
    def _():
        attention(True, image, set_a)
        norm(True, image, set_a)

    kinds = len(outs)
    early_names, late_names = (0, 1), (2, 3)
    flows = [Flow(place, kind, *buffers[6 * kind : 6 * kind + 6], outs[kind], send_sem, recv_sem) for kind in range(kinds)]
    own_early, own_late = [flow.own for flow in flows[:2]], [flow.own for flow in flows[2:]]

    def sizes_of(names):
        return [(name, flows[name].own.shape[0] * flows[name].own.shape[1] * flows[name].dtype.itemsize) for name in names]

    later_steps = images - early_images
    table, rest = planned(sizes_of(early_names), sizes_of(late_names), (PAIRS + 1) * later_steps, place.blocks)

    @pl.when(encoder & (step < half))
    def _():
        branch_back(True, 2 * step, *branch_args)

    def start_reduce():
        put_columns(own_early[:1], 0, [acc_r[:, at : at + width].astype(bf16).T for at in range(0, acc_r.shape[1], width)])
        flows[0].advance(0)

    @pl.when(encoder & (step == half - 1))
    def _():
        pl.semaphore_wait(barrier, 1 + len(others))
        start_reduce()

    @pl.when(encoder & (step < half))
    def _():
        feed_forward_back(True, 2 * step, *first_args)
        feed_forward_gradients(True, 2 * step, *weight_args)

    @pl.when(decoder & (step < half))
    def _():
        branch_back(False, 2 * step, *branch_args)
        feed_forward_back(False, 2 * step, *first_args)
        attention(False, 2 * step, pair_a)
        norm(False, 2 * step, pair_a)
        attention(False, 2 * step + 1, pair_b)
        norm(False, 2 * step + 1, pair_b)
        feed_forward_gradients(False, 2 * step, *weight_args)
        joint_gradient()

    @pl.when(decoder & (step == 0))
    def _():
        pl.semaphore_wait(barrier, 1 + len(others))

    @pl.when(decoder & (step < half))
    def _():
        code_copy(2 * step).start()
        code_copy(2 * step + 1).start()

    @pl.when(decoder & (step == half - 1))
    def _():
        start_reduce()

    def point(number):
        for name, turn in table[number]:
            if turn > 0:
                flows[name].advance(turn)

    @pl.when(step == half)
    def _():
        ff = acc_e.shape[1]
        rest_of = own_early[1].shape[1] - ff - width
        put_columns(own_early[1:], 0, [acc_e[...].astype(bf16), acc_m[...].astype(bf16), jnp.zeros((width, rest_of), bf16)])
        flows[1].advance(0)

    for number in range(PAIRS + 1):
        for later in range(later_steps):
            @pl.when(step == half + later)
            def _(later=later, number=number):
                point((PAIRS + 1) * later + number)

        if number < PAIRS:
            @pl.when(encoder & (step >= half))
            def _(number=number):
                attention(True, image, set_a, (number,))

    @pl.when(encoder & (step >= half))
    def _():
        norm(True, image, set_a)

    @pl.when(step == steps - 1)
    def _():
        first = own_late[0].shape[1]
        own_late[0][...] = acc_j[:, :first].astype(bf16)
        flows[2].advance(0)
        for index in range(hidden_sums.shape[1] // width):
            vectors[EXPAND_BIAS + index : EXPAND_BIAS + index + 1] = hidden_sums[:, index * width : (index + 1) * width]
        cuts = range(0, width, LANES)
        lat, rows = latent_sums[...].astype(bf16), vectors[...].astype(bf16)
        lat = jnp.concatenate([lat[:, at : at + LANES] for at in cuts], 0)
        rows = jnp.concatenate([rows[:, at : at + LANES] for at in cuts], 0)
        rows = jnp.concatenate([rows, jnp.zeros((width - rows.shape[0], LANES), bf16)], 0)
        put_columns(own_late[1:], 0, [acc_j[:, first:].astype(bf16), lat, rows, jnp.zeros((width, LANES), bf16)])
        flows[3].advance(0)
        for name, turn in rest:
            if turn > 0:
                flows[name].advance(turn)
        for flow in flows:
            flow.drain()
        for index in range(max(0, images - slots), images):
            rows_copy(index).wait()

    @pl.when((step == steps - 1) & decoder)
    def _():
        for index in range(images):
            code_copy(index).wait_send()


def finish_kernel(
    early_0, early_1, late_0, late_1, lat_columns, small_ref, rows_ref,
    wr_ref, we_ref, wj_ref, wm_ref, grad_ref, lat_ref, map_ref, be_ref, g1_ref, b1_ref, bm_ref, g2_ref, b2_ref, br_ref,
):
    width, ff = wm_ref.shape[2], we_ref.shape[2]
    early, late = (early_0, early_1), (late_0, late_1)
    grad_ref[...] = rows_ref[...].astype(f32)
    for index in range(ff // width):
        wr_ref[index] = columns(early, index * width, (index + 1) * width).astype(f32)
    we_ref[0] = columns(early, ff, 2 * ff).astype(f32)
    wm_ref[0] = columns(early, 2 * ff, 2 * ff + width).astype(f32)
    wj_ref[0] = columns(late, 0, 3 * width).astype(f32)

    @pl.when(pl.program_id(0) == 0)
    def _():
        spread = small_ref[...].astype(f32)

        def row(number):
            cuts = [spread[2 * CODE_ROWS * index + number : 2 * CODE_ROWS * index + number + 1] for index in range(width // LANES)]
            return jnp.concatenate(cuts, 1)

        tall = lat_ref.shape[1]
        for index in range(width // LANES):
            spot = lat_columns[index * tall : (index + 1) * tall]
            lat_ref[0, :, index * LANES : (index + 1) * LANES] = spot.astype(f32)
        for index in range(map_ref.shape[0]):
            map_ref[index] = row(LATENT_MAP + index)
        for piece in range(ff // width):
            be_ref[:, piece * width : (piece + 1) * width] = row(EXPAND_BIAS + piece)
        for number, ref in (
            (FIRST_GAIN, g1_ref), (FIRST_BIAS, b1_ref), (MIXER_BIAS, bm_ref), (SECOND_GAIN, g2_ref), (SECOND_BIAS, b2_ref),
            (REDUCE_BIAS, br_ref),
        ):
            ref[...] = row(number)


def whole(shape):
    return pl.BlockSpec(shape, lambda i: (0,) * len(shape), pipeline_mode=pl.Buffered(1))


def total(shape):
    return pl.BlockSpec(shape, lambda i: (0,) * len(shape))


def each(shape):
    return pl.BlockSpec((1,) + shape, lambda i: (i,) + (0,) * len(shape))


def each_second(shape):
    return pl.BlockSpec((1, 1) + shape, lambda i: (0, i) + (0,) * len(shape))


def sds(shape, dtype):
    return jax.ShapeDtypeStruct(shape, dtype)


def per_device(
    sizes, rows_in, rows_cot, counts, codes, codebook, first_gain, first_bias, joint_weight, mixer_weight, mixer_bias,
    second_gain, second_bias, expand_weight, expand_bias, reduce_weight, reduce_bias, latent_rows, latent_map,
):
    images, patch, width = rows_in.shape[1:]
    latents, code_width = latent_rows.shape[1], latent_map.shape[2]
    rows, ff = patch + latents, expand_weight.shape[2]
    entries = codebook.shape[0]
    map_cols = latent_map[0].T
    n = images
    half = n // 2
    scalars = pl.BlockSpec(memory_space=pltpu.SMEM)
    hbm = pl.BlockSpec(memory_space=pl.ANY)
    vec, wide = whole((1, width)), whole((1, ff))
    wj_spec, wm_spec = whole((1, width, 3 * width)), whole((1, width, width))
    we_spec, wr_spec = whole((1, width, ff)), whole((1, ff, width))
    saved = pl.pallas_call(
        forward_kernel,
        grid=(n,),
        in_specs=[
            scalars, each_second((patch, width)), whole((n, latents)), whole((latents, width)), whole((code_width, width)),
            whole((code_width, entries)),
            vec, vec, wj_spec, wm_spec, vec, vec, vec, we_spec, wide, wr_spec, vec,
        ],
        out_specs=[
            each_second((patch, width)), each((rows, 3 * width)), each((HEADS, rows, rows)), each((rows, width)), each((rows, width)),
            each((rows, width)), each((rows, LANES)), each((rows, width)), each((rows, ff)), each((rows, ff)),
            each((latents, width)), each((CODE_ROWS, latents)),
        ],
        out_shape=[
            sds((1, n, patch, width), bf16), sds((n, rows, 3 * width), bf16), sds((n, HEADS, rows, rows), bf16),
            sds((n, rows, width), bf16), sds((n, rows, width), bf16), sds((n, rows, width), bf16), sds((n, rows, LANES), f32),
            sds((n, rows, width), bf16), sds((n, rows, ff), bf16), sds((n, rows, ff), bf16),
            sds((n, latents, width), bf16), sds((n, CODE_ROWS, latents), f32),
        ],
        scratch_shapes=[
            pltpu.VMEM((CODE_ROWS, width), bf16), pltpu.VMEM((entries // GROUP * 3 * CODE_ROWS, GROUP), bf16),
            pltpu.VMEM((CODE_ROWS, 2 * latents), f32),
        ],
        compiler_params=pltpu.CompilerParams(vmem_limit_bytes=VMEM_BYTES),
        name="forward",
    )(
        counts, rows_in, codes, latent_rows[0], map_cols, codebook.T,
        first_gain, first_bias, joint_weight, mixer_weight, mixer_bias,
        second_gain, second_bias, expand_weight, expand_bias, reduce_weight, reduce_bias,
    )
    rows_out, joint, e, rl, mixed, x1, rs, x2, act, dg, latlow, small = saved

    def two(shape):
        return pl.BlockSpec((2,) + shape, lambda i: (jnp.minimum(i, half - 1),) + (0,) * len(shape))

    early = ahead(n)

    def first_of(shape):
        def index(i):
            mine = jnp.maximum(i - half + early, 0)
            return (jnp.where(lax.axis_index("section") == 0, mine, jnp.minimum(2 * i, n - 2)),) + (0,) * len(shape)

        return pl.BlockSpec((1,) + shape, index)

    def second_of(shape):
        def index(i):
            return (jnp.where(lax.axis_index("section") == 0, 1, jnp.minimum(2 * i + 1, n - 1)),) + (0,) * len(shape)

        return pl.BlockSpec((1,) + shape, index)

    shapes = [
        (rows, 3 * width), (HEADS, rows, rows), (rows, width), (rows, width), (rows, width), (rows, LANES), (CODE_ROWS, latents),
    ]
    shared = shapes[:4]
    pair, side, line, blocks = sizes
    ring = min(n, n - early)
    spans = (ff, ff + width + LANES, 2 * width, 2 * width)

    def flow_scratch(height, span, dtype):
        span, short = span // pair, height // side
        far = (blocks, short // line, span) if blocks > 1 else (1, 16, LANES)
        return [
            pltpu.VMEM((height, span * pair), dtype), pltpu.VMEM((height, span), dtype), pltpu.VMEM((short, span), dtype),
            pltpu.VMEM((max(1, line - 1), short // line, span), dtype), pltpu.VMEM(far, dtype),
            pltpu.VMEM((height, span * pair), dtype),
        ]

    flow_count = len(spans)
    rows_grad, *flow_sums = pl.pallas_call(
        functools.partial(backward_kernel, sizes),
        grid=(half + n - early,),
        in_specs=[
            scalars, pl.BlockSpec((1, 2, patch, width), lambda i: (0, jnp.minimum(i, half - 1), 0, 0)), two((rows, ff)),
            two((rows, ff)), two((rows, width)), two((rows, LANES)), two((rows, width)), two((latents, width)),
            two((CODE_ROWS, latents)),
            *[first_of(shape) for shape in shapes], *[second_of(shape) for shape in shared],
            whole((code_width, width)), vec, vec, wj_spec, wm_spec, vec, vec, we_spec, wr_spec,
        ],
        out_specs=[hbm] * (flow_count + 1),
        out_shape=[sds((1, n, patch, width), bf16)] + [sds((width, span), bf16) for span in spans],
        scratch_shapes=[
            pltpu.VMEM((width, ff), f32), pltpu.VMEM((width, ff), f32), pltpu.VMEM((width, 3 * width), f32),
            pltpu.VMEM((width, width), f32), pltpu.VMEM((2 * CODE_ROWS, width), f32), pltpu.VMEM((1, ff), f32),
            pltpu.VMEM((latents, width), f32),
            pltpu.VMEM((ring, rows, width), bf16), pltpu.VMEM((ring, rows, width), bf16),
            pltpu.VMEM((2 * rows, ff), bf16), pltpu.VMEM((2 * rows, width), bf16), pltpu.VMEM((2, width, 2 * rows), bf16), pltpu.VMEM((2, rows, 3 * width), bf16), pltpu.VMEM((2, width, rows), bf16),
            pltpu.VMEM((2, patch, width), bf16), pltpu.VMEM((CODE_ROWS, width), bf16),
            pltpu.VMEM((n, CODE_ROWS, latents), f32), pltpu.VMEM((n, CODE_ROWS, latents), f32),
            pltpu.SemaphoreType.DMA((n,)), pltpu.SemaphoreType.DMA((n,)), pltpu.SemaphoreType.DMA((n,)),
            pltpu.SemaphoreType.DMA((flow_count, 14)), pltpu.SemaphoreType.DMA((flow_count, 14)),
        ] + [ref for span in spans for ref in flow_scratch(width, span, bf16)],
        compiler_params=pltpu.CompilerParams(vmem_limit_bytes=VMEM_BYTES, collective_id=1, has_side_effects=True),
        name="backward",
    )(
        counts, rows_cot, act, dg, x2, rs, mixed, latlow, small,
        joint, e, rl, x1, mixed, rs, small, joint, e, rl, x1,
        map_cols, first_gain, first_bias, joint_weight, mixer_weight, second_gain, second_bias, expand_weight, reduce_weight,
    )

    parts = 4
    per = n // parts if n % parts == 0 else n
    quarter = width // parts
    vec_out, wide_out = total((1, width)), total((1, ff))

    def part(span):
        return pl.BlockSpec((quarter, span), lambda i: (i, 0))

    def out_part(height, span):
        return pl.BlockSpec((1, height, span), lambda i: (0, i, 0))

    images_part = pl.BlockSpec((1, per, patch, width), lambda i: (0, i % (n // per), 0, 0))
    wr, we, wj, wm, rows_grad, glat, gmap, gbe, g1, b1, bm, g2, b2, br = pl.pallas_call(
        finish_kernel,
        grid=(parts,),
        in_specs=[
            *[part(span) for span in spans], pl.BlockSpec((width, LANES), lambda i: (0, spans[-1] // LANES - 3)),
            pl.BlockSpec((width, LANES), lambda i: (0, spans[-1] // LANES - 2)),
            images_part,
        ],
        out_specs=[
            pl.BlockSpec((ff // width, quarter, width), lambda i: (0, i, 0)), out_part(quarter, ff), out_part(quarter, 3 * width), out_part(quarter, width),
            images_part, total((1, latents, width)), total((code_width, 1, width)), wide_out,
            vec_out, vec_out, vec_out, vec_out, vec_out, vec_out,
        ],
        out_shape=[
            sds((ff // width, width, width), f32), sds((1, width, ff), f32), sds((1, width, 3 * width), f32), sds((1, width, width), f32),
            sds((1, n, patch, width), f32), sds((1, latents, width), f32), sds((code_width, 1, width), f32), sds((1, ff), f32),
        ] + [sds((1, width), f32)] * 6,
        compiler_params=pltpu.CompilerParams(vmem_limit_bytes=VMEM_BYTES),
        name="finish",
    )(*flow_sums, flow_sums[-1], flow_sums[-1], rows_grad)
    gmap = jnp.transpose(gmap, (1, 2, 0))
    wr = wr.reshape(1, ff, width)
    return (rows_out, rows_grad, g1, b1, wj, wm, bm, g2, b2, we, gbe, wr, br, glat, gmap)


def solution(mesh):
    stacked, matrix = P("section", None), P("section", None, None)
    rows = P("section", "dp", None, None)
    placed = (
        rows, rows, P("dp"), P("dp", None), P(), stacked, stacked, matrix, matrix, stacked, stacked, stacked, matrix,
        stacked, matrix, stacked, matrix, matrix,
    )
    given = (
        rows, rows, stacked, stacked, matrix, matrix, stacked, stacked, stacked, matrix, stacked, matrix, stacked, matrix, matrix,
    )
    body = functools.partial(per_device, reach(mesh.shape["dp"]))
    return jax.shard_map(body, mesh=mesh, in_specs=placed, out_specs=given, check_vma=False)
```
